32 devices in a mesh: shard: 8 (over z, x), replica: 4 (over y, core).
Axes of the slice: x: 2, y: 2, z: 4, core: 2. Of those that a mesh axis runs over, the one named last changes fastest.
Arguments:
- kv_grads: bfloat16 [32, 2, 2048, 1024], P(('shard', 'replica')), may hold values from -28800 to 28800
- router_grads: bfloat16 [32, 2, 2048, 8], P(('shard', 'replica')), may hold values from -1536 to 1536
- gain_grads: bfloat16 [32, 2, 2, 2048], P(('shard', 'replica')), may hold values from -1536 to 1536
- kv_master: float32 [2048, 1024], P('shard'), may hold values from -1.5 to 1.5
- kv_first: float32 [2048, 1024], P('shard'), may hold values from -4 to 4
- kv_second: float32 [2048, 1024], P('shard'), may hold values from 0.05 to 2
- router_master: float32 [2048, 8], P('shard'), may hold values from -1.5 to 1.5
- router_first: float32 [2048, 8], P('shard'), may hold values from -4 to 4
- router_second: float32 [2048, 8], P('shard'), may hold values from 0.05 to 2
- gains: float32 [2, 2048], P(None, 'shard'), may hold values from 0.5 to 1.5
- gains_first: float32 [2, 2048], P(None, 'shard'), may hold values from -4 to 4
- gains_second: float32 [2, 2048], P(None, 'shard'), may hold values from 0.05 to 2
Outputs:
- kv_master_new: float32 [2048, 1024], P('shard')
- kv_first_new: float32 [2048, 1024], P('shard')
- kv_second_new: float32 [2048, 1024], P('shard')
- router_master_new: float32 [2048, 8], P('shard')
- router_first_new: float32 [2048, 8], P('shard')
- router_second_new: float32 [2048, 8], P('shard')
- gains_new: float32 [2, 2048], P(None, 'shard')
- gains_first_new: float32 [2, 2048], P(None, 'shard')
- gains_second_new: float32 [2, 2048], P(None, 'shard')
- kv_full: bfloat16 [2048, 1024], replicated
The draws below stay inside these ranges and needn't reach their ends.
All inputs are finite; a program needn't handle non-finite values.
Results may differ from the reference program's by a relative error of at most 0.0004.
Values may be sent and summed in bfloat16 or wider, within the bound.
A program may use at most 64 MiB of HBM per device.

```python
import math
import jax
import jax.numpy as jnp
from jax import lax

D = 2048
EXPERTS = 8
MB = 2
STEP = 10
KV = 512
GROUP = 8
WORKERS = 32
PARAMS = 2117632


def draw_kv_grads(key, part):
    key_rows = jax.random.fold_in(key, 11)
    key_cols = jax.random.fold_in(key, 12)
    key_pair = jax.random.fold_in(key, 13)
    key_main = jax.random.fold_in(key, 14)
    rise = 3.0
    position = jnp.arange(D, dtype=jnp.float32) / jnp.float32(D - 1)
    row_scale = jnp.exp(jnp.log(rise) * position + jnp.log(10.0) * jax.random.uniform(key_rows, (D,), jnp.float32))
    col_scale = jnp.exp(jnp.log(10.0) * jax.random.uniform(key_cols, (2 * KV,), jnp.float32))
    pairing = jax.random.permutation(key_pair, WORKERS) % GROUP
    row_block = jnp.arange(D) // (D // GROUP)

    def one_worker(worker):
        worker_key = jax.random.fold_in(key_main, worker)
        noise = jnp.clip(jax.random.normal(worker_key, (MB, D, 2 * KV), jnp.float32), -4.0, 4.0)
        boost = jnp.where(row_block == pairing[worker], 6.0, 1.0).astype(jnp.float32)
        values = noise * boost[None, :, None] * row_scale[None, :, None] * col_scale[None, None, :]
        return values.astype(jnp.bfloat16)
    return lax.map(one_worker, jnp.arange(WORKERS))


def raised(drawn, stream_key, source, target, blocks, factor):
    def block_of(dim):
        return (jnp.arange(drawn.shape[dim]) // (drawn.shape[dim] // blocks)).reshape((-1,) + (1,) * (drawn.ndim - 1 - dim))

    first = jax.random.permutation(stream_key, blocks)[block_of(target)]
    far = (block_of(target) + blocks // 2) % blocks
    return jnp.where((block_of(source) == first) | (block_of(source) == far), factor * drawn, drawn)


def block_scale(rng, dims, cuts, low, top_value):
    level, own = 1.0, jax.random.fold_in(rng, 6)
    for dim, shards_of in cuts:
        steps = jnp.exp(jax.random.uniform(jax.random.fold_in(own, dim), (shards_of,), jnp.float32, low / len(cuts), top_value / len(cuts)))
        level = level * jnp.repeat(steps, dims[dim] // shards_of).reshape([-1 if axis == dim else 1 for axis in range(len(dims))])
    return level


def scatter_about(rng, shape, spread, limit, pieces=(), kind=jnp.bfloat16):
    drawn = spread * jax.random.normal(rng, shape, jnp.float32)
    if pieces:
        drawn = drawn * block_scale(rng, shape, pieces, -0.22, 0.18)
    return jnp.clip(drawn, -limit, limit).astype(kind)


def noise_with(rng, dims, scale, most, cuts, heavy, held_as=jnp.bfloat16):
    result = scale * jax.random.normal(rng, dims, jnp.float32)
    if cuts:
        result = result * block_scale(rng, dims, cuts, -0.22, 0.18)
    return jnp.clip(raised(result, jax.random.fold_in(rng, 3), *heavy), -most, most).astype(held_as)


def setup_inputs(seed: int = 0) -> dict:
    key_list = jax.random.split(jax.random.key(seed), 13)
    kv_grads = draw_kv_grads(jax.random.fold_in(key_list[12], 71), 0)
    router_grads = noise_with(key_list[1], (WORKERS, MB, D, EXPERTS), 128.0, 1536.0, ((0, 32),), (0, 2, 32, 2.75))
    gain_grads = noise_with(key_list[2], (WORKERS, MB, 2, D), 128.0, 1536.0, ((0, 32),), (0, 3, 32, 2.75))
    kv_master = scatter_about(key_list[3], (D, 2 * KV), 0.1, 1.5, ((0, 8),), jnp.float32)
    kv_first = scatter_about(key_list[4], (D, 2 * KV), 0.3, 4.0, ((0, 8),), jnp.float32)
    kv_second = jnp.clip(jnp.exp(math.log(2.0) - 3.6888794 * jax.random.uniform(key_list[5], (D, 2 * KV), jnp.float32) ** block_scale(key_list[5], (D, 2 * KV), ((0, 8),), -0.2, 0.2)), 0.05, 2.0)
    router_master = scatter_about(key_list[6], (D, EXPERTS), 0.1, 1.5, ((0, 8),), jnp.float32)
    router_first = scatter_about(key_list[7], (D, EXPERTS), 0.3, 4.0, ((0, 8),), jnp.float32)
    router_second = jnp.clip(jnp.exp(math.log(2.0) - 3.6888794 * jax.random.uniform(key_list[8], (D, EXPERTS), jnp.float32) ** block_scale(key_list[8], (D, EXPERTS), ((0, 8),), -0.2, 0.2)), 0.05, 2.0)
    gains = jnp.clip(1.0 + 0.1 * jax.random.normal(key_list[9], (2, D), jnp.float32), 0.5, 1.5)
    gains_first = scatter_about(key_list[10], (2, D), 0.3, 4.0, ((1, 8),), jnp.float32)
    gains_second = jnp.clip(jnp.exp(math.log(2.0) - 3.6888794 * jax.random.uniform(key_list[11], (2, D), jnp.float32) ** block_scale(key_list[11], (2, D), ((1, 8),), -0.2, 0.2)), 0.05, 2.0)
    return dict(kv_grads=kv_grads, router_grads=router_grads, gain_grads=gain_grads, kv_master=kv_master, kv_first=kv_first, kv_second=kv_second, router_master=router_master, router_first=router_first, router_second=router_second, gains=gains, gains_first=gains_first, gains_second=gains_second)


beta_one = 0.9
beta_two = 0.95
learning_rate = 0.01
adam_eps = 1e-08

def adamw(master, first, second, gradient, weight_decay):
    first_new = beta_one * first + (1.0 - beta_one) * gradient
    second_new = beta_two * second + (1.0 - beta_two) * gradient * gradient
    direction = first_new / (1.0 - beta_one ** STEP) / (jnp.sqrt(second_new / (1.0 - beta_two ** STEP)) + adam_eps)
    master_new = master - learning_rate * (direction + weight_decay * master)
    return (master_new, first_new, second_new)

def reference(kv_grads, router_grads, gain_grads, kv_master, kv_first, kv_second, router_master, router_first, router_second, gains, gains_first, gains_second):

    def add_worker(running, worker_piece):
        return (running + lax.optimization_barrier(jnp.sum(worker_piece.astype(jnp.float32), axis=0)), None)
    kv_sum, _ = lax.scan(add_worker, jnp.zeros((D, 2 * KV), jnp.float32), kv_grads)
    router_sum = lax.optimization_barrier(jnp.sum(router_grads.astype(jnp.float32), axis=(0, 1)))
    gain_sum = lax.optimization_barrier(jnp.sum(gain_grads.astype(jnp.float32), axis=(0, 1)))
    sum_squares = jnp.sum(kv_sum * kv_sum) + jnp.sum(router_sum * router_sum) + jnp.sum(gain_sum * gain_sum)
    clip_factor = jnp.minimum(jnp.float32(1.0), jnp.sqrt(jnp.float32(PARAMS)) / (jnp.sqrt(sum_squares) + 1e-06))
    kv_new, kv_first_new, kv_second_new = adamw(kv_master, kv_first, kv_second, clip_factor * kv_sum, 0.1)
    router_new, router_first_new, router_second_new = adamw(router_master, router_first, router_second, clip_factor * router_sum, 0.1)
    gains_new, gains_first_new, gains_second_new = adamw(gains, gains_first, gains_second, clip_factor * gain_sum, 0.0)
    return (kv_new, kv_first_new, kv_second_new, router_new, router_first_new, router_second_new, gains_new, gains_first_new, gains_second_new, kv_new.astype(jnp.bfloat16))
```

```python
import functools
import jax
import jax.numpy as jnp
from jax import lax
from jax.experimental import pallas as pl
from jax.experimental.pallas import tpu as pltpu
from jax.sharding import PartitionSpec as P

STEP = 10
PARAMS = 2117632
CHUNKS = 2

beta_one = 0.9
beta_two = 0.95
learning_rate = 0.01
adam_eps = 1e-08


def adamw(master, first, second, gradient, weight_decay):
    first_new = beta_one * first + (1.0 - beta_one) * gradient
    second_new = beta_two * second + (1.0 - beta_two) * gradient * gradient
    direction = (
        first_new
        / (1.0 - beta_one**STEP)
        / (jnp.sqrt(second_new / (1.0 - beta_two**STEP)) + adam_eps)
    )
    master_new = master - learning_rate * (direction + weight_decay * master)
    return (master_new, first_new, second_new)


def encode(x):
    return ((x * jnp.abs(x)) * (x * x)).astype(jnp.bfloat16)


def decode(code):
    y = code.astype(jnp.float32)
    size = jnp.abs(y)
    x = lax.rsqrt(lax.rsqrt(size))
    x = jnp.where(y < 0, -x, x)
    return jnp.where(size < 2e-38, 0.0, x)


def bit(value, j):
    return lax.rem(lax.div(value, 2**j), 2)


def flipped(value, other, width):
    out = 0
    for j in range(width):
        out = out + lax.rem(bit(value, j) + bit(other, j), 2) * 2**j
    return out


def orders(shard_bits, replica_bits):
    shards = [("shard", j) for j in range(shard_bits)]
    replicas = [("replica", j) for j in range(replica_bits)]
    one = [replicas[0], shards[0]] + replicas[1:] + shards[1:]
    two = replicas + shards
    return (one, two)


def kernel(
    shards, replicas,
    kv_grads, router_grads, gain_grads, master, first, second,
    r_master, r_first, r_second, g_master, g_first, g_second,
    master_out, first_out, second_out, rm_out, rf_out, rs_out, gm_out, gf_out, gs_out, full,
    slabs, acc, outgoing, incoming, whole_sum, own,
    small, small_in, small_out, square_out, square_in,
    load_sem, cut_send, cut_recv, small_send, small_recv, join_send, join_recv,
    square_send, square_recv, up_sem, down_sem, x_sem, pair_sem, local_sem,
):
    s, r = lax.axis_index("shard"), lax.axis_index("replica")
    rows, columns = master.shape
    width = columns // (CHUNKS * replicas)
    small_width = r_master.shape[1]
    shard_bits, replica_bits = shards.bit_length() - 1, replicas.bit_length() - 1
    bits = shard_bits + replica_bits
    blocks = shards * replicas
    plan = orders(shard_bits, replica_bits)
    step = min(rows, 64)
    pieces = [pl.ds(i * step, step) for i in range(rows // step)]

    def partner(axis, j):
        if axis == "shard":
            return {"shard": s + (1 - 2 * bit(s, j)) * 2**j, "replica": r}
        return {"shard": s, "replica": r + (1 - 2 * bit(r, j)) * 2**j}

    def remote(src, dst, send, recv, device):
        return pltpu.make_async_remote_copy(
            src_ref=src, dst_ref=dst, send_sem=send, recv_sem=recv,
            device_id=device, device_id_type=pl.DeviceIdType.MESH,
        )

    def load(offset):
        owner = flipped(s, offset, shard_bits)
        return pltpu.make_async_copy(
            kv_grads.at[:, pl.ds(pl.multiple_of(owner * rows, rows), rows), :],
            slabs.at[offset], load_sem.at[offset],
        )

    pl.loop(0, shards)(lambda offset: load(offset).start())

    lines = shards // 2
    z, x = lax.div(s, 2), lax.rem(s, 2)
    barrier = pltpu.get_barrier_semaphore()
    for axis, j in plan[0]:
        pl.semaphore_signal(
            barrier, inc=1, device_id=partner(axis, j), device_id_type=pl.DeviceIdType.MESH
        )
    above, below = {"shard": s + 2, "replica": r}, {"shard": s - 2, "replica": r}

    @pl.when(z < lines - 1)
    def _():
        pl.semaphore_signal(barrier, inc=1, device_id=above, device_id_type=pl.DeviceIdType.MESH)

    @pl.when(z > 0)
    def _():
        pl.semaphore_signal(barrier, inc=1, device_id=below, device_id_type=pl.DeviceIdType.MESH)

    def column_of(chunk, offset):
        owner = flipped(r, offset, replica_bits)
        return pl.ds(pl.multiple_of((chunk * replicas + owner) * width, width), width)

    def place(chunk, shard_offset, replica_offset):
        out = 0
        for k, (axis, j) in enumerate(plan[chunk]):
            out = out + bit(shard_offset if axis == "shard" else replica_offset, j) * (
                blocks >> (k + 1)
            )
        return out

    def prepare(chunk, sent):
        def body(offset):
            for q in range(replicas):
                if q % 2 != sent:
                    continue
                at = place(chunk, offset, q)
                cols = column_of(chunk, q)
                for piece in pieces:
                    value = slabs[offset, 0, piece, cols].astype(jnp.float32) + slabs[
                        offset, 1, piece, cols
                    ].astype(jnp.float32)
                    if sent:
                        outgoing[chunk, at, piece, :] = encode(value)
                    else:
                        acc[chunk, at, piece, :] = value

        pl.loop(0, shards)(body)

    def cut(chunk, k):
        half = blocks >> (k + 1)
        axis, j = plan[chunk][k]
        return remote(
            outgoing.at[chunk, pl.ds(half, half)], incoming.at[chunk, pl.ds(half, half)],
            cut_send.at[chunk, k], cut_recv.at[chunk, k], partner(axis, j),
        )

    pl.loop(0, shards)(lambda offset: load(offset).wait())
    prepare(0, 1)
    pl.semaphore_wait(
        barrier, bits + jnp.where(z < lines - 1, 1, 0) + jnp.where(z > 0, 1, 0)
    )
    cut(0, 0).start()
    prepare(1, 1)
    cut(1, 0).start()

    small_plan = [("shard", j) for j in range(shard_bits)] + [
        ("replica", j) for j in range(replica_bits)
    ]

    def small_place(offset):
        out = 0
        for k in range(shard_bits):
            out = out + bit(offset, k) * (shards >> (k + 1))
        return out

    def small_body(offset):
        owner = flipped(s, offset, shard_bits)
        at = small_place(offset)
        small[at] = jnp.zeros((16, small_width), jnp.float32)

        def taken(ref):
            if small_width % 128 == 0:
                cols = pl.ds(pl.multiple_of(owner * small_width, small_width), small_width)
                return ref[0, :, cols].astype(jnp.float32) + ref[1, :, cols].astype(jnp.float32)
            total = ref[0].astype(jnp.float32) + ref[1].astype(jnp.float32)
            out = jnp.zeros((total.shape[0], small_width), jnp.float32)
            for i in range(shards):
                out = jnp.where(owner == i, total[:, i * small_width : (i + 1) * small_width], out)
            return out

        small[at, 0:8, :] = taken(router_grads)
        small[at, 8:10, :] = taken(gain_grads)

    pl.loop(0, shards)(small_body)

    def small_copy(k):
        axis, j = small_plan[k]
        if k < shard_bits:
            half = shards >> (k + 1)
            return remote(
                small.at[pl.ds(half, half)], small_in.at[pl.ds(half, half)],
                small_send.at[k], small_recv.at[k], partner(axis, j),
            )
        i = k - shard_bits
        return remote(
            small_out.at[i], small_in.at[shards + i],
            small_send.at[k], small_recv.at[k], partner(axis, j),
        )

    small_copy(0).start()
    prepare(0, 0)
    prepare(1, 0)

    def take(chunk, k):
        half = blocks >> (k + 1)
        cut(chunk, k).wait_recv()
        rest = half // 2

        def send_body(i):
            for piece in pieces:
                outgoing[chunk, i, piece, :] = encode(
                    acc[chunk, i, piece, :] + decode(incoming[chunk, half + i, piece, :])
                )

        def keep_body(i):
            for piece in pieces:
                acc[chunk, i, piece, :] += decode(incoming[chunk, half + i, piece, :])

        if rest:
            pl.loop(rest, half)(send_body)
            cut(chunk, k + 1).start()
            pl.loop(0, rest)(keep_body)
        else:
            for piece in pieces:
                whole_sum[chunk, 0, piece, :] = acc[chunk, 0, piece, :] + decode(
                    incoming[chunk, half, piece, :]
                )

    def take_small(k):
        small_copy(k).wait_recv()
        if k < shard_bits:
            half = shards >> (k + 1)

            def body(i):
                small[i] += small_in[half + i]

            pl.loop(0, half)(body)
            if k == shard_bits - 1:
                small_out[0] = small[0]
        else:
            i = k - shard_bits
            small_out[i + 1] = small_out[i] + small_in[shards + i]
        if k < bits - 1:
            small_copy(k + 1).start()

    join_bits = list(reversed(range(replica_bits)))

    def join(chunk, i):
        known = 2**i
        return remote(
            whole_sum.at[chunk, pl.ds(0, known)], whole_sum.at[chunk, pl.ds(known, known)],
            join_send.at[chunk, i], join_recv.at[chunk, i], partner("replica", join_bits[i]),
        )

    for k in range(bits):
        for chunk in range(CHUNKS):
            take(chunk, k)
            if k == bits - 1:
                join(chunk, 0).start()
        take_small(k)

    def folded(value):
        return jnp.sum(value.reshape(-1, 8, 128), axis=0)

    squares = jnp.zeros((8, 128), jnp.float32)
    for chunk in range(CHUNKS):
        for piece in pieces:
            value = whole_sum[chunk, 0, piece, :]
            squares = squares + folded(value * value)
    small_sum = small_out[replica_bits]
    squares = squares + jnp.sum(small_sum * small_sum) * (1.0 / (replicas * 8 * 128))
    square_out[0] = squares

    def square_copy(k):
        axis, j = small_plan[k]
        return remote(
            square_out.at[k], square_in.at[k], square_send.at[k], square_recv.at[k],
            partner(axis, j),
        )

    for k in range(bits):
        square_copy(k).start()
        square_copy(k).wait_recv()
        square_out[k + 1] = square_out[k] + square_in[k]
    for i in range(1, replica_bits):
        for chunk in range(CHUNKS):
            join(chunk, i - 1).wait_recv()
            join(chunk, i).start()

    total = jnp.broadcast_to(jnp.sum(square_out[bits], keepdims=True), (8, 128))
    clip = jnp.minimum(
        1.0, jnp.sqrt(jnp.full((8, 128), PARAMS, jnp.float32)) / (jnp.sqrt(total) + 1e-06)
    )
    clip = clip[0:1, 0:1]

    rm_out[...], rf_out[...], rs_out[...] = adamw(
        r_master[...], r_first[...], r_second[...], clip * small_sum[0:8], 0.1
    )
    gm_out[...], gf_out[...], gs_out[...] = adamw(
        g_master[...], g_first[...], g_second[...], clip * small_sum[8:10], 0.0
    )

    def replica_offset(at):
        out = 0
        for i, j in enumerate(join_bits):
            out = out + ((at >> i) % 2) * 2**j
        return out

    for at in range(replicas):
        for chunk in range(CHUNKS):
            if at == replicas // 2:
                join(chunk, replica_bits - 1).wait_recv()
            cols = column_of(chunk, replica_offset(at))
            for piece in pieces:
                new, first_new, second_new = adamw(
                    master[piece, cols], first[piece, cols], second[piece, cols],
                    clip * whole_sum[chunk, at, piece, :], 0.1,
                )
                master_out[piece, cols] = new
                first_out[piece, cols] = first_new
                second_out[piece, cols] = second_new
                own[piece, cols] = new.astype(jnp.bfloat16)

    side = lax.rem(r, 2)
    half_columns = columns // 2
    cols = pl.ds(pl.multiple_of(side * half_columns, half_columns), half_columns)
    pair, across = partner("replica", 0), partner("shard", 0)

    def block(zz, xx):
        return full.at[pl.ds(pl.multiple_of((zz * 2 + xx) * rows, rows), rows), cols]

    def up(t):
        src = own.at[:, cols] if isinstance(t, int) else block(z - t, x)
        return remote(src, block(z - t, x), up_sem.at[0, t], up_sem.at[1, t], above)

    def down(t):
        src = own.at[:, cols] if isinstance(t, int) else block(z + t, x)
        return remote(src, block(z + t, x), down_sem.at[0, t], down_sem.at[1, t], below)

    def cross(role, zz):
        src = own.at[:, cols] if isinstance(role, int) else block(zz, x)
        return remote(src, block(zz, x), x_sem.at[0, role], x_sem.at[1, role], across)

    def to_pair(which, role, zz, xx):
        return remote(
            block(zz, xx), block(zz, xx),
            pair_sem.at[0, which, role], pair_sem.at[1, which, role], pair,
        )

    mine = pltpu.make_async_copy(
        own, full.at[pl.ds(pl.multiple_of(s * rows, rows), rows)], local_sem
    )

    @pl.when(z < lines - 1)
    def _():
        up(0).start()

    @pl.when(z > 0)
    def _():
        down(0).start()

    cross(0, z).start()
    mine.start()
    cross(0, z).wait_recv()
    to_pair(1, 0, z, 1 - x).start()

    def walk(t):
        @pl.when(z - t >= 0)
        def _():
            up(t - 1).wait_recv()

            @pl.when(z < lines - 1)
            def _():
                up(t).start()

            cross(t, z - t).start()
            to_pair(0, t, z - t, x).start()

        @pl.when(z + t < lines)
        def _():
            down(t - 1).wait_recv()

            @pl.when(z > 0)
            def _():
                down(t).start()

            cross(lines + t, z + t).start()
            to_pair(0, lines + t, z + t, x).start()

        @pl.when(z - t >= 0)
        def _():
            cross(t, z - t).wait_recv()
            to_pair(1, t, z - t, 1 - x).start()

        @pl.when(z + t < lines)
        def _():
            cross(lines + t, z + t).wait_recv()
            to_pair(1, lines + t, z + t, 1 - x).start()

    pl.loop(1, lines)(walk)

    mine.wait()
    cross(0, z).wait_send()
    to_pair(1, 0, z, 1 - x).wait()

    @pl.when(z < lines - 1)
    def _():
        up(0).wait_send()

    @pl.when(z > 0)
    def _():
        down(0).wait_send()

    def settle(t):
        @pl.when(z - t >= 0)
        def _():
            @pl.when(z < lines - 1)
            def _():
                up(t).wait_send()

            cross(t, z - t).wait_send()
            to_pair(0, t, z - t, x).wait()
            to_pair(1, t, z - t, 1 - x).wait()

        @pl.when(z + t < lines)
        def _():
            @pl.when(z > 0)
            def _():
                down(t).wait_send()

            cross(lines + t, z + t).wait_send()
            to_pair(0, lines + t, z + t, x).wait()
            to_pair(1, lines + t, z + t, 1 - x).wait()

    pl.loop(1, lines)(settle)
    for k in range(bits):
        for chunk in range(CHUNKS):
            cut(chunk, k).wait_send()
        small_copy(k).wait_send()
        square_copy(k).wait_send()
    for i in range(replica_bits):
        for chunk in range(CHUNKS):
            join(chunk, i).wait_send()


def on_device(
    shards, replicas,
    kv_grads, router_grads, gain_grads,
    kv_master, kv_first, kv_second,
    router_master, router_first, router_second,
    gains, gains_first, gains_second,
):
    rows, columns = kv_master.shape
    blocks = shards * replicas
    bits = blocks.bit_length() - 1
    replica_bits = replicas.bit_length() - 1
    width = columns // (CHUNKS * replicas)
    small_width = router_master.shape[0]
    lines = shards // 2
    f32, bf16 = jnp.float32, jnp.bfloat16
    shape = jax.ShapeDtypeStruct
    vmem, anywhere = pl.BlockSpec(memory_space=pltpu.VMEM), pl.BlockSpec(memory_space=pl.ANY)
    dma = pltpu.SemaphoreType.DMA
    outs = pl.pallas_call(
        functools.partial(kernel, shards, replicas),
        out_shape=[shape(kv_master.shape, f32)] * 3
        + [shape(router_master.shape[::-1], f32)] * 3
        + [shape(gains.shape, f32)] * 3
        + [shape((rows * shards, columns), bf16)],
        in_specs=[anywhere] + [vmem] * 11,
        out_specs=[vmem] * 9 + [anywhere],
        scratch_shapes=[
            pltpu.VMEM((shards, 2, rows, columns), bf16),
            pltpu.VMEM((CHUNKS, blocks // 2, rows, width), f32),
            pltpu.VMEM((CHUNKS, blocks, rows, width), bf16),
            pltpu.VMEM((CHUNKS, blocks, rows, width), bf16),
            pltpu.VMEM((CHUNKS, replicas, rows, width), f32),
            pltpu.VMEM((rows, columns), bf16),
            pltpu.VMEM((shards, 16, small_width), f32),
            pltpu.VMEM((shards + replica_bits, 16, small_width), f32),
            pltpu.VMEM((replica_bits + 1, 16, small_width), f32),
            pltpu.VMEM((bits + 1, 8, 128), f32),
            pltpu.VMEM((bits, 8, 128), f32),
            dma((shards,)),
            dma((CHUNKS, bits)), dma((CHUNKS, bits)),
            dma((bits,)), dma((bits,)),
            dma((CHUNKS, replica_bits)), dma((CHUNKS, replica_bits)),
            dma((bits,)), dma((bits,)),
            dma((2, lines)), dma((2, lines)),
            dma((2, 2 * lines)),
            dma((2, 2, 2 * lines)),
            dma,
        ],
        compiler_params=pltpu.CompilerParams(
            collective_id=0, has_side_effects=True, vmem_limit_bytes=52 * 2**20
        ),
    )(
        kv_grads[0], router_grads[0].transpose(0, 2, 1), gain_grads[0],
        kv_master, kv_first, kv_second,
        router_master.T, router_first.T, router_second.T,
        gains, gains_first, gains_second,
    )
    return (*outs[:3], *(out.T for out in outs[3:6]), *outs[6:])


def solution(mesh):
    kept, gain_split = P("shard", None), P(None, "shard")
    grads = P(("shard", "replica"), None, None, None)
    return jax.shard_map(
        functools.partial(on_device, mesh.shape["shard"], mesh.shape["replica"]),
        mesh=mesh,
        in_specs=(grads,) * 3 + (kept,) * 6 + (gain_split,) * 3,
        out_specs=(kept,) * 6 + (gain_split,) * 3 + (P(),),
        check_vma=False,
    )
```

```python
import functools
import jax
import jax.numpy as jnp
from jax import lax
from jax.experimental import pallas as pl
from jax.experimental.pallas import tpu as pltpu
from jax.sharding import PartitionSpec as P

STEP = 10
PARAMS = 2117632
CHUNKS = 2

beta_one = 0.9
beta_two = 0.95
learning_rate = 0.01
adam_eps = 1e-08


def adamw(master, first, second, gradient, weight_decay):
    first_new = beta_one * first + (1.0 - beta_one) * gradient
    second_new = beta_two * second + (1.0 - beta_two) * gradient * gradient
    direction = (
        first_new
        / (1.0 - beta_one**STEP)
        / (jnp.sqrt(second_new / (1.0 - beta_two**STEP)) + adam_eps)
    )
    master_new = master - learning_rate * (direction + weight_decay * master)
    return (master_new, first_new, second_new)


EDGE = 2.0**-8
JOINT = 2.0**-48


def encode(x, k):
    size = jnp.abs(x) * 2.0**-k
    second = size * size
    fourth = second * second
    code = jnp.where(size >= EDGE, fourth * fourth, second * JOINT)
    return jnp.where(x < 0, -code, code).astype(jnp.bfloat16)


def decode(code, k):
    y = code.astype(jnp.float32)
    size = jnp.abs(y)
    root = lax.rsqrt(size)
    fourth = lax.rsqrt(root)
    high = fourth * lax.rsqrt(fourth) * 2.0**k
    low = size * root * (JOINT**-0.5 * 2.0**k)
    x = jnp.where(size >= EDGE**8, high, low)
    x = jnp.where(y < 0, -x, x)
    return jnp.where(size < 2e-38, 0.0, x)


def bit(value, j):
    return lax.rem(lax.div(value, 2**j), 2)


def flipped(value, other, width):
    out = 0
    for j in range(width):
        out = out + lax.rem(bit(value, j) + bit(other, j), 2) * 2**j
    return out


def orders(shard_bits, replica_bits):
    shards = [("shard", j) for j in range(shard_bits)]
    replicas = [("replica", j) for j in range(replica_bits)]
    one = [replicas[0]] + shards[:2] + replicas[1:] + shards[2:]
    two = replicas + shards
    return (one, two)


def kernel(
    shards, replicas,
    kv_grads, router_grads, gain_grads, master_in, first_in, second_in,
    kv_gradient, small_gradient, full,
    slabs, acc, outgoing, incoming, whole_sum, own, master, first, second, routers, gain_rows,
    small, small_in, small_out, square_r, square_s,
    load_sem, state_sem, cut_send, cut_recv, small_send, small_recv, join_send, join_recv,
    square_r_sem, square_s_sem, up_sem, down_sem, x_sem, pair_sem, local_sem,
):
    s, r = lax.axis_index("shard"), lax.axis_index("replica")
    rows, columns = master.shape
    width = columns // (CHUNKS * replicas)
    small_width = small.shape[2]
    shard_bits, replica_bits = shards.bit_length() - 1, replicas.bit_length() - 1
    bits = shard_bits + replica_bits
    blocks = shards * replicas
    plan = orders(shard_bits, replica_bits)
    step = min(rows, 64)
    pieces = [pl.ds(i * step, step) for i in range(rows // step)]

    def partner(axis, j):
        if axis == "shard":
            return {"shard": s + (1 - 2 * bit(s, j)) * 2**j, "replica": r}
        return {"shard": s, "replica": r + (1 - 2 * bit(r, j)) * 2**j}

    def remote(src, dst, send, recv, device):
        return pltpu.make_async_remote_copy(
            src_ref=src, dst_ref=dst, send_sem=send, recv_sem=recv,
            device_id=device, device_id_type=pl.DeviceIdType.MESH,
        )

    def load(offset):
        owner = flipped(s, offset, shard_bits)
        return pltpu.make_async_copy(
            kv_grads.at[:, pl.ds(pl.multiple_of(owner * rows, rows), rows), :],
            slabs.at[offset], load_sem.at[offset],
        )

    pl.loop(0, shards)(lambda offset: load(offset).start())

    def fetch(i):
        pairs = (
            (router_grads, routers), (gain_grads, gain_rows),
            (master_in, master), (first_in, first), (second_in, second),
        )
        return pltpu.make_async_copy(pairs[i][0], pairs[i][1], state_sem.at[i])

    for i in range(5):
        fetch(i).start()

    lines = shards // 2
    z, x = lax.div(s, 2), lax.rem(s, 2)
    above, below = {"shard": s + 2, "replica": r}, {"shard": s - 2, "replica": r}

    def shard_peer(d):
        return {"shard": lax.rem(s + d, shards), "replica": r}

    def replica_peer(d):
        return {"shard": s, "replica": lax.rem(r + d, replicas)}

    barrier = pltpu.get_barrier_semaphore()

    def greet(device):
        pl.semaphore_signal(
            barrier, inc=1, device_id=device, device_id_type=pl.DeviceIdType.MESH
        )

    pl.loop(1, replicas)(lambda d: greet(replica_peer(d)))
    pl.loop(1, shards)(lambda d: greet(shard_peer(d)))

    def column_of(chunk, offset):
        owner = flipped(r, offset, replica_bits)
        at = lax.rem(owner, 2) * (columns // 2) + (
            chunk * (replicas // 2) + lax.div(owner, 2)
        ) * width
        return pl.ds(pl.multiple_of(at, width), width)

    def place(chunk, shard_offset, replica_offset):
        out = 0
        for k, (axis, j) in enumerate(plan[chunk]):
            out = out + bit(shard_offset if axis == "shard" else replica_offset, j) * (
                blocks >> (k + 1)
            )
        return out

    def prepare(chunk, sent, arriving=False):
        def body(offset):
            if arriving:
                load(offset).wait()
            for q in range(replicas):
                if q % 2 != sent:
                    continue
                at = place(chunk, offset, q)
                cols = column_of(chunk, q)
                for piece in pieces:
                    value = slabs[offset, 0, piece, cols].astype(jnp.float32) + slabs[
                        offset, 1, piece, cols
                    ].astype(jnp.float32)
                    if sent:
                        outgoing[chunk, at, piece, :] = encode(value, 0)
                    else:
                        acc[chunk, at, piece, :] = value

        pl.loop(0, shards)(body)

    def cut(chunk, k):
        half = blocks >> (k + 1)
        axis, j = plan[chunk][k]
        return remote(
            outgoing.at[chunk, pl.ds(half, half)], incoming.at[chunk, pl.ds(half, half)],
            cut_send.at[chunk, k], cut_recv.at[chunk, k], partner(axis, j),
        )

    prepare(0, 1, arriving=True)
    pl.semaphore_wait(barrier, shards + replicas - 2)
    cut(0, 0).start()
    prepare(1, 1)
    cut(1, 0).start()

    small_plan = [("shard", j) for j in range(shard_bits)] + [
        ("replica", j) for j in range(replica_bits)
    ]

    def small_place(offset):
        out = 0
        for k in range(shard_bits):
            out = out + bit(offset, k) * (shards >> (k + 1))
        return out

    def small_body(offset):
        owner = flipped(s, offset, shard_bits)
        at = small_place(offset)
        small[at] = jnp.zeros((16, small_width), jnp.float32)

        def taken(ref):
            if small_width % 128 == 0:
                cols = pl.ds(pl.multiple_of(owner * small_width, small_width), small_width)
                return ref[0, :, cols].astype(jnp.float32) + ref[1, :, cols].astype(jnp.float32)
            total = ref[0].astype(jnp.float32) + ref[1].astype(jnp.float32)
            out = jnp.zeros((total.shape[0], small_width), jnp.float32)
            for i in range(shards):
                out = jnp.where(owner == i, total[:, i * small_width : (i + 1) * small_width], out)
            return out

        small[at, 0:8, :] = taken(routers)
        small[at, 8:10, :] = taken(gain_rows)

    fetch(0).wait()
    fetch(1).wait()
    pl.loop(0, shards)(small_body)

    def small_copy(k):
        axis, j = small_plan[k]
        if k < shard_bits:
            half = shards >> (k + 1)
            return remote(
                small.at[pl.ds(half, half)], small_in.at[pl.ds(half, half)],
                small_send.at[k], small_recv.at[k], partner(axis, j),
            )
        i = k - shard_bits
        return remote(
            small_out.at[i], small_in.at[shards + i],
            small_send.at[k], small_recv.at[k], partner(axis, j),
        )

    small_copy(0).start()
    prepare(0, 0)
    prepare(1, 0)

    def take(chunk, k):
        half = blocks >> (k + 1)
        cut(chunk, k).wait_recv()
        rest = half // 2

        def send_body(i):
            for piece in pieces:
                outgoing[chunk, i, piece, :] = encode(
                    acc[chunk, i, piece, :] + decode(incoming[chunk, half + i, piece, :], k),
                    k + 1,
                )

        def keep_body(i):
            for piece in pieces:
                acc[chunk, i, piece, :] += decode(incoming[chunk, half + i, piece, :], k)

        if rest:
            pl.loop(rest, half)(send_body)
            cut(chunk, k + 1).start()
            pl.loop(0, rest)(keep_body)
        else:
            for piece in pieces:
                whole_sum[chunk, 0, piece, :] = acc[chunk, 0, piece, :] + decode(
                    incoming[chunk, half, piece, :], k
                )

    def take_small(k):
        small_copy(k).wait_recv()
        if k < shard_bits:
            half = shards >> (k + 1)

            def body(i):
                small[i] += small_in[half + i]

            pl.loop(0, half)(body)
            if k == shard_bits - 1:
                small_out[0] = small[0]
        else:
            i = k - shard_bits
            small_out[i + 1] = small_out[i] + small_in[shards + i]
        if k < bits - 1:
            small_copy(k + 1).start()

    join_bits = list(reversed(range(replica_bits)))

    def join(chunk, i):
        known = 2**i
        return remote(
            whole_sum.at[chunk, pl.ds(0, known)], whole_sum.at[chunk, pl.ds(known, known)],
            join_send.at[chunk, i], join_recv.at[chunk, i], partner("replica", join_bits[i]),
        )

    for k in range(bits):
        for chunk in range(CHUNKS):
            take(chunk, k)
            if k == bits - 1:
                join(chunk, 0).start()
        take_small(k)

    def folded(value):
        return jnp.sum(value.reshape(-1, 8, 128), axis=0)

    squares = jnp.zeros((8, 128), jnp.float32)
    for chunk in range(CHUNKS):
        for piece in pieces:
            value = whole_sum[chunk, 0, piece, :]
            squares = squares + folded(value * value)
    small_sum = small_out[replica_bits]
    squares = squares + jnp.sum(small_sum * small_sum) * (1.0 / (replicas * 8 * 128))

    def square_over_r(d):
        return remote(
            square_r.at[r], square_r.at[r], square_r_sem.at[0, d], square_r_sem.at[1, d],
            replica_peer(d),
        )

    def square_over_s(d):
        return remote(
            square_s.at[s], square_s.at[s], square_s_sem.at[0, d], square_s_sem.at[1, d],
            shard_peer(d),
        )

    square_r[r] = squares
    pl.loop(1, replicas)(lambda d: square_over_r(d).start())
    pl.loop(1, replicas)(lambda d: square_over_r(d).wait_recv())
    square_s[s] = jnp.sum(square_r[...], axis=0)
    pl.loop(1, shards)(lambda d: square_over_s(d).start())
    for i in range(1, replica_bits):
        for chunk in range(CHUNKS):
            join(chunk, i - 1).wait_recv()
            join(chunk, i).start()
    for i in range(2, 5):
        fetch(i).wait()
    pl.loop(1, shards)(lambda d: square_over_s(d).wait_recv())

    total = jnp.broadcast_to(
        jnp.sum(jnp.sum(square_s[...], axis=0), keepdims=True), (8, 128)
    )
    clip = jnp.minimum(
        1.0, jnp.sqrt(jnp.full((8, 128), PARAMS, jnp.float32)) / (jnp.sqrt(total) + 1e-06)
    )
    clip = clip[0:1, 0:1]

    def replica_offset(at):
        out = 0
        for i, j in enumerate(join_bits):
            out = out + ((at >> i) % 2) * 2**j
        return out

    for at in range(replicas // 2):
        for chunk in range(CHUNKS):
            q = replica_offset(at)
            cols = column_of(chunk, q)
            owner = flipped(r, q, replica_bits)
            inside = (chunk * (replicas // 2) + lax.div(owner, 2)) * width
            inside = pl.ds(pl.multiple_of(inside, width), width)
            for piece in pieces:
                new, _, _ = adamw(
                    master[piece, cols], first[piece, cols], second[piece, cols],
                    clip * whole_sum[chunk, at, piece, :], 0.1,
                )
                own[piece, inside] = new.astype(jnp.bfloat16)

    side = lax.rem(r, 2)
    half_columns = columns // 2
    cols = pl.ds(pl.multiple_of(side * half_columns, half_columns), half_columns)
    pair, across = partner("replica", 0), partner("shard", 0)

    def block(zz, xx):
        return full.at[pl.ds(pl.multiple_of((zz * 2 + xx) * rows, rows), rows), cols]

    def up(t):
        src = own if isinstance(t, int) else block(z - t, x)
        return remote(src, block(z - t, x), up_sem.at[0, t], up_sem.at[1, t], above)

    def down(t):
        src = own if isinstance(t, int) else block(z + t, x)
        return remote(src, block(z + t, x), down_sem.at[0, t], down_sem.at[1, t], below)

    def cross(role, zz):
        src = own if isinstance(role, int) else block(zz, x)
        return remote(src, block(zz, x), x_sem.at[0, role], x_sem.at[1, role], across)

    def to_pair(which, role, zz, xx):
        src = own if isinstance(role, int) and which == 0 else block(zz, xx)
        return remote(
            src, block(zz, xx),
            pair_sem.at[0, which, role], pair_sem.at[1, which, role], pair,
        )

    mine = pltpu.make_async_copy(own, block(z, x), local_sem)

    @pl.when(z < lines - 1)
    def _():
        up(0).start()

    @pl.when(z > 0)
    def _():
        down(0).start()

    cross(0, z).start()
    to_pair(0, 0, z, x).start()
    mine.start()

    small_gradient[...] = clip * small_sum
    for at in range(replicas):
        for chunk in range(CHUNKS):
            if at == replicas // 2:
                join(chunk, replica_bits - 1).wait_recv()
            gradient_cols = column_of(chunk, replica_offset(at))
            for piece in pieces:
                kv_gradient[piece, gradient_cols] = clip * whole_sum[chunk, at, piece, :]

    cross(0, z).wait_recv()
    to_pair(1, 0, z, 1 - x).start()

    def walk(t):
        @pl.when(z - t >= 0)
        def _():
            up(t - 1).wait_recv()

            @pl.when(z < lines - 1)
            def _():
                up(t).start()

            cross(t, z - t).start()
            to_pair(0, t, z - t, x).start()

        @pl.when(z + t < lines)
        def _():
            down(t - 1).wait_recv()

            @pl.when(z > 0)
            def _():
                down(t).start()

            cross(lines + t, z + t).start()
            to_pair(0, lines + t, z + t, x).start()

        @pl.when(z - t >= 0)
        def _():
            cross(t, z - t).wait_recv()
            to_pair(1, t, z - t, 1 - x).start()

        @pl.when(z + t < lines)
        def _():
            cross(lines + t, z + t).wait_recv()
            to_pair(1, lines + t, z + t, 1 - x).start()

    pl.loop(1, lines)(walk)

    mine.wait()
    cross(0, z).wait_send()
    to_pair(0, 0, z, x).wait()
    to_pair(1, 0, z, 1 - x).wait()

    @pl.when(z < lines - 1)
    def _():
        up(0).wait_send()

    @pl.when(z > 0)
    def _():
        down(0).wait_send()

    def settle(t):
        @pl.when(z - t >= 0)
        def _():
            @pl.when(z < lines - 1)
            def _():
                up(t).wait_send()

            cross(t, z - t).wait_send()
            to_pair(0, t, z - t, x).wait()
            to_pair(1, t, z - t, 1 - x).wait()

        @pl.when(z + t < lines)
        def _():
            @pl.when(z > 0)
            def _():
                down(t).wait_send()

            cross(lines + t, z + t).wait_send()
            to_pair(0, lines + t, z + t, x).wait()
            to_pair(1, lines + t, z + t, 1 - x).wait()

    pl.loop(1, lines)(settle)
    for k in range(bits):
        for chunk in range(CHUNKS):
            cut(chunk, k).wait_send()
        small_copy(k).wait_send()
    for i in range(replica_bits):
        for chunk in range(CHUNKS):
            join(chunk, i).wait_send()
    pl.loop(1, replicas)(lambda d: square_over_r(d).wait_send())
    pl.loop(1, shards)(lambda d: square_over_s(d).wait_send())


def on_device(
    shards, replicas,
    kv_grads, router_grads, gain_grads,
    kv_master, kv_first, kv_second,
    router_master, router_first, router_second,
    gains, gains_first, gains_second,
):
    rows, columns = kv_master.shape
    blocks = shards * replicas
    bits = blocks.bit_length() - 1
    replica_bits = replicas.bit_length() - 1
    width = columns // (CHUNKS * replicas)
    small_width = router_master.shape[0]
    lines = shards // 2
    f32, bf16 = jnp.float32, jnp.bfloat16
    shape = jax.ShapeDtypeStruct
    vmem, anywhere = pl.BlockSpec(memory_space=pltpu.VMEM), pl.BlockSpec(memory_space=pl.ANY)
    dma = pltpu.SemaphoreType.DMA
    state = pltpu.VMEM((rows, columns), f32)
    kv_gradient, small_gradient, kv_full = pl.pallas_call(
        functools.partial(kernel, shards, replicas),
        out_shape=[
            shape(kv_master.shape, f32),
            shape((16, small_width), f32),
            shape((rows * shards, columns), bf16),
        ],
        in_specs=[anywhere] * 6,
        out_specs=[vmem, vmem, anywhere],
        scratch_shapes=[
            pltpu.VMEM((shards, 2, rows, columns), bf16),
            pltpu.VMEM((CHUNKS, blocks // 2, rows, width), f32),
            pltpu.VMEM((CHUNKS, blocks, rows, width), bf16),
            pltpu.VMEM((CHUNKS, blocks, rows, width), bf16),
            pltpu.VMEM((CHUNKS, replicas, rows, width), f32),
            pltpu.VMEM((rows, columns // 2), bf16),
            state, state, state,
            pltpu.VMEM((2,) + router_grads.shape[:1:-1], bf16),
            pltpu.VMEM(gain_grads.shape[1:], bf16),
            pltpu.VMEM((shards, 16, small_width), f32),
            pltpu.VMEM((shards + replica_bits, 16, small_width), f32),
            pltpu.VMEM((replica_bits + 1, 16, small_width), f32),
            pltpu.VMEM((replicas, 8, 128), f32),
            pltpu.VMEM((shards, 8, 128), f32),
            dma((shards,)), dma((5,)),
            dma((CHUNKS, bits)), dma((CHUNKS, bits)),
            dma((bits,)), dma((bits,)),
            dma((CHUNKS, replica_bits)), dma((CHUNKS, replica_bits)),
            dma((2, replicas)), dma((2, shards)),
            dma((2, lines)), dma((2, lines)),
            dma((2, 2 * lines)),
            dma((2, 2, 2 * lines)),
            dma,
        ],
        compiler_params=pltpu.CompilerParams(
            collective_id=0, has_side_effects=True, vmem_limit_bytes=60 * 2**20
        ),
    )(
        kv_grads[0], router_grads[0].transpose(0, 2, 1), gain_grads[0],
        kv_master, kv_first, kv_second,
    )
    experts = router_master.shape[1]
    kv = adamw(kv_master, kv_first, kv_second, kv_gradient, 0.1)
    router = adamw(
        router_master, router_first, router_second, small_gradient[:experts].T, 0.1
    )
    gain = adamw(
        gains, gains_first, gains_second, small_gradient[experts : experts + 2], 0.0
    )
    return (*kv, *router, *gain, kv_full)


def solution(mesh):
    kept, gain_split = P("shard", None), P(None, "shard")
    grads = P(("shard", "replica"), None, None, None)
    return jax.shard_map(
        functools.partial(on_device, mesh.shape["shard"], mesh.shape["replica"]),
        mesh=mesh,
        in_specs=(grads,) * 3 + (kept,) * 6 + (gain_split,) * 3,
        out_specs=(kept,) * 6 + (gain_split,) * 3 + (P(),),
        check_vma=False,
    )
```
